32 devices in a mesh: ctx: 4 (over x, core), head: 8 (over z, y).
Axes of the slice: x: 2, y: 2, z: 4, core: 2. Of those that a mesh axis runs over, the one named last changes fastest.
Arguments:
- tokens: bfloat16 [1024, 8192], P('ctx', 'head'), may hold values from -6 to 6
- out_grad: bfloat16 [1024, 8192], P('ctx', 'head'), may hold values from -6 to 6
- w_query: bfloat16 [8192, 4096], P(None, 'head'), may hold values from -0.0625 to 0.0625
- w_key: bfloat16 [8192, 4096], P(None, 'head'), may hold values from -0.0625 to 0.0625
- w_value: bfloat16 [8192, 4096], P(None, 'head'), may hold values from -0.0625 to 0.0625
- w_output: bfloat16 [8192, 4096], P(None, 'head'), may hold values from -0.09375 to 0.09375
Outputs:
- input_grad: bfloat16 [1024, 8192], P('ctx', 'head')
- grad_query: bfloat16 [8192, 4096], P('ctx', 'head')
- grad_key: bfloat16 [8192, 4096], P('ctx', 'head')
- grad_value: bfloat16 [8192, 4096], P('ctx', 'head')
- grad_output: bfloat16 [8192, 4096], P('ctx', 'head')
The draws below stay inside these ranges and needn't reach their ends.
All inputs are finite; a program needn't handle non-finite values.
Results may differ from the reference program's by a relative error of at most 0.017.
Values may be sent and summed in bfloat16 or wider, within the bound.
No kernel may reach another device: no remote copies, remote signals or barrier semaphores. Data moves between devices by JAX's collectives and lax.ppermute only.
A program may use at most 256 MiB of HBM per device.

```python
import jax
import jax.numpy as jnp
from jax import lax

D = 8192
HD = 128
HEADS = 32
TOK_DEV = 256
INNER = 4096
TOKENS = 1024
N_CTX = 4


def steps_of(key, shape, cuts, least, largest):
    level, own = 1.0, jax.random.fold_in(key, 6)
    for position, parts in cuts:
        steps = jnp.exp(jax.random.uniform(jax.random.fold_in(own, position), (parts,), jnp.float32, least / len(cuts), largest / len(cuts)))
        level = level * jnp.repeat(steps, shape[position] // parts).reshape([-1 if axis == position else 1 for axis in range(len(shape))])
    return level


def bell_draw(stream_key, dims, scale, most, cuts=(), held_as=jnp.bfloat16):
    values = jax.random.normal(stream_key, dims, jnp.float32) * scale
    if len(cuts) > 0:
        values = steps_of(stream_key, dims, cuts, -0.22, 0.18) * values
    return jnp.clip(values, min=-most, max=most).astype(held_as)


def setup_inputs(seed: int = 0) -> dict:
    arg_keys = jax.random.split(jax.random.key(seed), 7)
    tokens = bell_draw(arg_keys[0], (TOKENS, D), 1.0, 6.0, ((0, 4), (1, 8)))
    out_grad = bell_draw(arg_keys[1], (TOKENS, D), 1.0, 6.0, ((0, 4), (1, 8)))
    w_query = bell_draw(arg_keys[2], (D, INNER), D ** -0.5, 0.0625, ((1, 8),))
    w_key = bell_draw(arg_keys[3], (D, INNER), D ** -0.5, 0.0625, ((1, 8),))
    w_value = bell_draw(arg_keys[4], (D, INNER), D ** -0.5, 0.0625, ((1, 8),))
    w_output = bell_draw(arg_keys[5], (D, INNER), INNER ** -0.5, 0.09375, ((1, 8),))
    return dict(tokens=tokens, out_grad=out_grad, w_query=w_query, w_key=w_key, w_value=w_value, w_output=w_output)


def feature(values):
    return jnp.where(values > 0, values + 1.0, jnp.exp(jnp.minimum(values, 0.0)))

def slope(values):
    return jnp.where(values > 0, 1.0, jnp.exp(jnp.minimum(values, 0.0)))

def rounded(values):
    return lax.optimization_barrier(values.astype(jnp.bfloat16)).astype(jnp.float32)

def reference(tokens, out_grad, w_query, w_key, w_value, w_output):
    highest = lax.Precision.HIGHEST
    blocks = N_CTX
    width = TOK_DEV
    total_heads = HEADS

    def split(values):
        return values.astype(jnp.float32).reshape(blocks, width, total_heads, HD).transpose(0, 2, 1, 3)

    def join(values):
        return values.transpose(0, 2, 1, 3).reshape(blocks * width, total_heads * HD)
    query_lin = jnp.dot(tokens, w_query, preferred_element_type=jnp.float32)
    key_lin = jnp.dot(tokens, w_key, preferred_element_type=jnp.float32)
    query_feat = split(feature(query_lin).astype(jnp.bfloat16))
    key_feat = split(feature(key_lin).astype(jnp.bfloat16))
    value_feat = split(jnp.dot(tokens, w_value, preferred_element_type=jnp.float32).astype(jnp.bfloat16))
    causal = jnp.tril(jnp.ones((width, width), dtype=bool))
    scores = rounded(jnp.where(causal, jnp.einsum('chtd,chsd->chts', query_feat, key_feat, precision=highest), 0.0))
    block_kv = jnp.einsum('chtd,chte->chde', key_feat, value_feat, precision=highest)
    zeros = jnp.zeros_like(block_kv[:1])
    prefix = jnp.concatenate([zeros, jnp.cumsum(block_kv[:-1], axis=0)], axis=0)
    attended = jnp.einsum('chts,chse->chte', scores, value_feat, precision=highest)
    attended = attended + jnp.einsum('chtd,chde->chte', query_feat, prefix, precision=highest)
    scale = lax.rsqrt(lax.optimization_barrier(jnp.mean(attended * attended, axis=-1, keepdims=True)) + 1e-06)
    normed = attended * scale
    attn_rows = join(normed).astype(jnp.bfloat16)
    attn_grad = split(jnp.dot(out_grad, w_output, preferred_element_type=jnp.float32))
    out_delta = rounded(scale * (attn_grad - normed * lax.optimization_barrier(jnp.mean(attn_grad * normed, axis=-1, keepdims=True))))
    block_qg = jnp.einsum('chtd,chte->chde', query_feat, out_delta, precision=highest)
    reversed_sums = jnp.cumsum(block_qg[::-1][:-1], axis=0)
    suffix = jnp.concatenate([reversed_sums[::-1], zeros], axis=0)
    score_grad = rounded(jnp.where(causal, jnp.einsum('chte,chse->chts', out_delta, value_feat, precision=highest), 0.0))
    feat_q = jnp.einsum('chts,chsd->chtd', score_grad, key_feat, precision=highest)
    feat_q = feat_q + jnp.einsum('chte,chde->chtd', out_delta, prefix, precision=highest)
    feat_k = jnp.einsum('chts,chtd->chsd', score_grad, query_feat, precision=highest)
    feat_k = feat_k + jnp.einsum('chse,chde->chsd', value_feat, suffix, precision=highest)
    feat_v = jnp.einsum('chts,chte->chse', scores, out_delta, precision=highest)
    feat_v = feat_v + jnp.einsum('chsd,chde->chse', key_feat, suffix, precision=highest)
    query_pre = (join(feat_q) * slope(query_lin)).astype(jnp.bfloat16)
    key_pre = (join(feat_k) * slope(key_lin)).astype(jnp.bfloat16)
    value_pre = join(feat_v).astype(jnp.bfloat16)
    input_grad = jnp.dot(query_pre, w_query.T, preferred_element_type=jnp.float32)
    input_grad = input_grad + jnp.dot(key_pre, w_key.T, preferred_element_type=jnp.float32)
    input_grad = input_grad + jnp.dot(value_pre, w_value.T, preferred_element_type=jnp.float32)

    def block_sum(left, right):
        total = jnp.zeros((left.shape[1], right.shape[1]), jnp.float32)
        for block in range(blocks):
            lower = block * width
            left_rows = left[lower:lower + width]
            right_rows = right[lower:lower + width]
            total = total + rounded(jnp.dot(left_rows.T, right_rows, preferred_element_type=jnp.float32))
        return total.astype(jnp.bfloat16)
    return (input_grad.astype(jnp.bfloat16), block_sum(tokens, query_pre), block_sum(tokens, key_pre), block_sum(tokens, value_pre), block_sum(out_grad, attn_rows))
```

```python
import jax
import jax.numpy as jnp
from jax import lax
from jax.sharding import PartitionSpec as P

HD = 128
F32 = jnp.float32
BF16 = jnp.bfloat16


def feature(values):
    return jnp.where(values > 0, values + 1.0, jnp.exp(jnp.minimum(values, 0.0)))


def slope(values):
    return jnp.where(values > 0, 1.0, jnp.exp(jnp.minimum(values, 0.0)))


def split_heads(values, number):
    return values.reshape(values.shape[0], number, HD).transpose(1, 0, 2)


def merge_heads(values):
    return values.transpose(1, 0, 2).reshape(values.shape[1], -1)


def ein(spec, left, right):
    return jnp.einsum(spec, left, right, preferred_element_type=F32)


class Lines:
    def __init__(self):
        self.nh = lax.axis_size("head")
        self.nc = lax.axis_size("ctx")
        self.Z = 4 if self.nh % 4 == 0 else 1
        self.Y = self.nh // self.Z
        here = lax.axis_index("head")
        self.c = lax.axis_index("ctx")
        self.z = here // self.Y
        self.y = here % self.Y

    def along_z(self, x):
        return lax.ppermute(x, "head", [(i, (i + self.Y) % self.nh) for i in range(self.nh)])

    def along_y(self, x):
        Y = self.Y
        return lax.ppermute(x, "head", [(i, i // Y * Y + (i + 1) % Y) for i in range(self.nh)])

    def across(self, x, j):
        return lax.ppermute(x, "ctx", [(i, i ^ j) for i in range(self.nc)])

    def shard(self, k, j):
        return ((self.z - k) % self.Z) * self.Y + (self.y - j) % self.Y


def gather_features(at, x):
    rows, cols = x.shape
    parts = []
    now = x
    for k in range(at.Z):
        if k:
            now = at.along_z(now)
        side = now
        for j in range(at.Y):
            if j:
                side = at.along_y(side)
            parts.append((at.shard(k, j), side))
    whole = jnp.zeros((rows, cols * at.nh), x.dtype)
    for place, part in parts:
        whole = lax.dynamic_update_slice(whole, part, (0, place * cols))
    return whole


def by_slices(at, whole):
    width = whole.shape[1] // at.nc
    out = []
    for j in range(at.nc):
        piece = lax.dynamic_slice_in_dim(whole, (at.c ^ j) * width, width, 1)
        out.append(at.across(piece, j) if j else piece)
    return jnp.concatenate(out, axis=0)


def by_blocks(at, x):
    return jnp.concatenate([at.across(x, j) if j else x for j in range(at.nc)], axis=0)


def states(at, x, later):
    every = lax.all_gather(x.astype(BF16), "ctx").astype(F32)
    index = jnp.arange(at.nc)
    keep = (index > at.c) if later else (index < at.c)
    return jnp.sum(jnp.where(keep[:, None, None, None], every, 0.0), axis=0)


def local(tokens, out_grad, w_query, w_key, w_value, w_output):
    at = Lines()
    length, cols = tokens.shape
    number = w_query.shape[1] // HD
    whole_tokens = gather_features(at, tokens)
    whole_grads = gather_features(at, out_grad)
    query_lin = jnp.dot(whole_tokens, w_query, preferred_element_type=F32)
    key_lin = jnp.dot(whole_tokens, w_key, preferred_element_type=F32)
    value_lin = jnp.dot(whole_tokens, w_value, preferred_element_type=F32)
    token_slices = by_slices(at, whole_tokens)
    grad_slices = by_slices(at, whole_grads)
    query_feat = split_heads(feature(query_lin).astype(BF16), number)
    key_feat = split_heads(feature(key_lin).astype(BF16), number)
    value_feat = split_heads(value_lin.astype(BF16), number)
    causal = lax.broadcasted_iota(jnp.int32, (length, length), 0) >= lax.broadcasted_iota(
        jnp.int32, (length, length), 1
    )
    scores = jnp.where(causal, ein("htd,hsd->hts", query_feat, key_feat), 0.0).astype(BF16)
    local_kv = ein("htd,hte->hde", key_feat, value_feat)
    prefix = states(at, local_kv, False).astype(BF16)
    attended = ein("hts,hse->hte", scores, value_feat) + ein("htd,hde->hte", query_feat, prefix)
    scale = lax.rsqrt(jnp.mean(attended * attended, axis=-1, keepdims=True) + 1e-06)
    normed = attended * scale
    attn_rows = merge_heads(normed).astype(BF16)
    rows_all = by_blocks(at, attn_rows)
    attn_grad = split_heads(jnp.dot(whole_grads, w_output, preferred_element_type=F32), number)
    out_delta = (
        scale * (attn_grad - normed * jnp.mean(attn_grad * normed, axis=-1, keepdims=True))
    ).astype(BF16)
    local_qg = ein("htd,hte->hde", query_feat, out_delta)
    suffix = states(at, local_qg, True).astype(BF16)
    score_grad = jnp.where(causal, ein("hte,hse->hts", out_delta, value_feat), 0.0).astype(BF16)
    feat_q = ein("hts,hsd->htd", score_grad, key_feat) + ein("hte,hde->htd", out_delta, prefix)
    feat_k = ein("hts,htd->hsd", score_grad, query_feat) + ein("hse,hde->hsd", value_feat, suffix)
    feat_v = ein("hts,hte->hse", scores, out_delta) + ein("hsd,hde->hse", key_feat, suffix)
    query_pre = (merge_heads(feat_q) * slope(query_lin)).astype(BF16)
    key_pre = (merge_heads(feat_k) * slope(key_lin)).astype(BF16)
    value_pre = merge_heads(feat_v).astype(BF16)
    pre = jnp.concatenate([query_pre, key_pre, value_pre], axis=1)

    def part(place):
        def term(left, w):
            rows = lax.dynamic_slice_in_dim(w, place * cols, cols, 0)
            return ein("ti,di->td", left, rows)

        return term(query_pre, w_query) + term(key_pre, w_key) + term(value_pre, w_value)

    total = None
    for k in range(1, at.Z + 1):
        held = None
        for j in range(1, at.Y + 1):
            mine = part(at.shard(k, j))
            held = mine if held is None else mine + held.astype(F32)
            if j < at.Y:
                held = at.along_y(held.astype(BF16))
        total = held if total is None else held + total.astype(F32)
        if k < at.Z:
            total = at.along_z(total.astype(BF16))
    input_grad = total.astype(BF16)
    pre_all = by_blocks(at, pre)
    width = query_pre.shape[1]
    weight_grads = ein("td,ti->di", token_slices, pre_all).astype(BF16)
    grad_query = weight_grads[:, :width]
    grad_key = weight_grads[:, width : 2 * width]
    grad_value = weight_grads[:, 2 * width :]
    grad_output = ein("td,ti->di", grad_slices, rows_all).astype(BF16)
    return (input_grad, grad_query, grad_key, grad_value, grad_output)


def solution(mesh):
    return jax.shard_map(
        local,
        mesh=mesh,
        in_specs=(P("ctx", "head"),) * 2 + (P(None, "head"),) * 4,
        out_specs=(P("ctx", "head"),) * 5,
        check_vma=False,
    )
```

```python
import functools

import jax
import jax.numpy as jnp
from jax import lax
from jax.experimental import pallas as pl
from jax.experimental.pallas import tpu as pltpu
from jax.sharding import PartitionSpec as P

HD = 128
F32 = jnp.float32
BF16 = jnp.bfloat16


def tie(x, *others):
    return lax.optimization_barrier((x,) + others)[0]


class Lines:
    def __init__(self):
        self.nh = lax.axis_size("head")
        self.nc = lax.axis_size("ctx")
        self.Z = 4 if self.nh % 4 == 0 else 1
        self.Y = self.nh // self.Z
        here = lax.axis_index("head")
        self.c = lax.axis_index("ctx")
        self.z = here // self.Y
        self.y = here % self.Y

    def along_z(self, x):
        return lax.ppermute(x, "head", [(i, (i + self.Y) % self.nh) for i in range(self.nh)])

    def along_y(self, x):
        Y = self.Y
        return lax.ppermute(x, "head", [(i, i // Y * Y + (i + 1) % Y) for i in range(self.nh)])

    def across(self, x, j):
        return lax.ppermute(x, "ctx", [(i, i ^ j) for i in range(self.nc)])

    def shard(self, k, j):
        return ((self.z - k) % self.Z) * self.Y + (self.y - j) % self.Y


def gather_piece(at, x, z_first, after=()):
    parts = []
    if z_first:
        now = x
        for k in range(at.Z):
            if k:
                now = at.along_z(tie(now, *after) if after and k == 1 else now)
            side = now
            for j in range(at.Y):
                if j:
                    side = at.along_y(side)
                parts.append((k, at.shard(k, j), side))
        return parts
    sides = [x]
    for _ in range(at.Y - 1):
        sides.append(at.along_y(sides[-1]))
    now = jnp.concatenate(sides, axis=1)
    cols = x.shape[1]
    for k in range(at.Z):
        if k:
            now = at.along_z(tie(now, *after) if after and k == 1 else now)
        for j in range(at.Y):
            parts.append((k, at.shard(k, j), now[:, j * cols : (j + 1) * cols]))
    return parts


def place(whole, parts, row, cols):
    for _, where, part in parts:
        whole = lax.dynamic_update_slice(whole, part, (row, where * cols))
    return whole


def slices_out(at, whole):
    width = whole.shape[1] // at.nc
    out = []
    for j in range(at.nc):
        piece = lax.dynamic_slice_in_dim(whole, (at.c ^ j) * width, width, 1)
        out.append(at.across(piece, j) if j else piece)
    return out


def blocks_out(at, x):
    return [at.across(x, j) if j else x for j in range(at.nc)]


def mm(a, b, ca, cb):
    return lax.dot_general(a, b, (((ca,), (cb,)), ((), ())), preferred_element_type=F32)


def slope(values):
    return jnp.where(values > 0, 1.0, jnp.exp(jnp.minimum(values, 0.0)))


def feature(values):
    return jnp.where(values > 0, values + 1.0, jnp.exp(jnp.minimum(values, 0.0)))


def causal(values):
    rows = lax.broadcasted_iota(jnp.int32, values.shape, 0)
    cols = lax.broadcasted_iota(jnp.int32, values.shape, 1)
    return jnp.where(rows >= cols, values, 0.0)


def per_head(kernel, number, ins, outs, scalars=(), flops=0):
    def spec(shape, kind):
        if kind == "c":
            return pl.BlockSpec((shape[0], HD), lambda h, *_: (0, h))
        if kind == "r":
            return pl.BlockSpec((shape[0] // number, shape[1]), lambda h, *_: (h, 0))
        return pl.BlockSpec((shape[0], shape[1], HD), lambda h, *_: (0, 0, h))

    arrays = [a for a, _ in ins]
    moved = sum(a.size * a.dtype.itemsize for a in arrays)
    shapes = [jax.ShapeDtypeStruct(s, d) for s, d, _ in outs]
    moved += sum(s.size * s.dtype.itemsize for s in shapes)
    return pl.pallas_call(
        kernel,
        out_shape=shapes,
        grid_spec=pltpu.PrefetchScalarGridSpec(
            num_scalar_prefetch=len(scalars),
            grid=(number,),
            in_specs=[spec(a.shape, k) for a, k in ins],
            out_specs=[spec(s, k) for s, _, k in outs],
        ),
        cost_estimate=pl.CostEstimate(flops=flops, bytes_accessed=moved, transcendentals=0),
    )(*scalars, *arrays)


def forward_kernel(q_ref, k_ref, v_ref, qf_ref, kf_ref, vf_ref, sc_ref, in_ref, kv_ref):
    qf = feature(q_ref[...]).astype(BF16)
    kf = feature(k_ref[...]).astype(BF16)
    vf = v_ref[...].astype(BF16)
    scores = causal(mm(qf, kf, 1, 1)).astype(BF16)
    qf_ref[...] = qf
    kf_ref[...] = kf
    vf_ref[...] = vf
    sc_ref[...] = scores
    in_ref[...] = mm(scores, vf, 1, 0)
    kv_ref[...] = mm(kf, vf, 0, 0).astype(BF16)


def state_sum(c, refs, later):
    total = jnp.zeros(refs[0].shape, F32)
    for j, ref in enumerate(refs):
        other = c ^ (j + 1)
        use = (other > c) if later else (other < c)
        total = total + jnp.where(use, ref[...].astype(F32), 0.0)
    return total.astype(BF16)


def norm_kernel(nc, c_ref, in_ref, qf_ref, *refs):
    kv, (no_ref, sl_ref, ar_ref, pf_ref) = refs[: nc - 1], refs[nc - 1 :]
    prefix = state_sum(c_ref[0], kv, False)
    attended = in_ref[...] + mm(qf_ref[...], prefix, 1, 0)
    scale = lax.rsqrt(jnp.mean(attended * attended, axis=1, keepdims=True) + 1e-06)
    normed = attended * scale
    no_ref[...] = normed
    sl_ref[...] = jnp.broadcast_to(scale, normed.shape)
    ar_ref[...] = normed.astype(BF16)
    pf_ref[...] = prefix


def delta_kernel(ga_ref, gb_ref, no_ref, sl_ref, qf_ref, od_ref, qg_ref):
    grad = ga_ref[...] + gb_ref[...]
    normed = no_ref[...]
    mean = jnp.mean(grad * normed, axis=1, keepdims=True)
    delta = (sl_ref[...] * (grad - normed * mean)).astype(BF16)
    od_ref[...] = delta
    qg_ref[...] = mm(qf_ref[...], delta, 0, 0).astype(BF16)


def inner_kernel(
    od_ref, qf_ref, kf_ref, vf_ref, sc_ref, pf_ref, q_ref, qp_ref, fk_ref, fv_ref
):
    delta = od_ref[...]
    score_grad = causal(mm(delta, vf_ref[...], 1, 1)).astype(BF16)
    feat_q = mm(score_grad, kf_ref[...], 1, 0) + mm(delta, pf_ref[...], 1, 1)
    qp_ref[...] = (feat_q * slope(q_ref[...])).astype(BF16)
    fk_ref[...] = mm(score_grad, qf_ref[...], 0, 0)
    fv_ref[...] = mm(sc_ref[...], delta, 0, 0)


def outer_kernel(nc, c_ref, fk_ref, fv_ref, kf_ref, vf_ref, k_ref, *refs):
    qg, (kv_ref,) = refs[: nc - 1], refs[nc - 1 :]
    suffix = state_sum(c_ref[0], qg, True)
    feat_k = fk_ref[...] + mm(vf_ref[...], suffix, 1, 1)
    feat_v = fv_ref[...] + mm(kf_ref[...], suffix, 1, 0)
    kv_ref[0] = (feat_k * slope(k_ref[...])).astype(BF16)
    kv_ref[1] = feat_v.astype(BF16)


def part_kernel(s_ref, q_ref, kv_ref, wq_ref, wk_ref, wv_ref, a_ref, b_ref):
    total = mm(q_ref[...], wq_ref[...], 1, 1)
    total = total + mm(kv_ref[0], wk_ref[...], 1, 1)
    total = total + mm(kv_ref[1], wv_ref[...], 1, 1)
    half = a_ref.shape[0]
    a_ref[...] = total[:half].astype(a_ref.dtype)
    b_ref[...] = total[half:].astype(b_ref.dtype)


def part_of(where, query_pre, kv_pre, weights, cols, dtype):
    rows, width = query_pre.shape
    tile = min(512, cols)
    count = cols // tile
    weight = pl.BlockSpec((tile, width), lambda i, s: (s[0] * count + i, 0))
    out = pl.BlockSpec((rows // 2, tile), lambda i, s: (0, i))
    return pl.pallas_call(
        part_kernel,
        out_shape=[jax.ShapeDtypeStruct((rows // 2, cols), dtype)] * 2,
        grid_spec=pltpu.PrefetchScalarGridSpec(
            num_scalar_prefetch=1,
            grid=(count,),
            in_specs=[
                pl.BlockSpec((rows, width), lambda i, s: (0, 0)),
                pl.BlockSpec((2, rows, width), lambda i, s: (0, 0, 0)),
                weight,
                weight,
                weight,
            ],
            out_specs=[out, out],
        ),
        cost_estimate=pl.CostEstimate(
            flops=6 * rows * width * cols, bytes_accessed=6 * cols * width, transcendentals=0
        ),
    )(jnp.reshape(where, (1,)).astype(jnp.int32), query_pre, kv_pre, *weights)


def local(tokens, out_grad, w_query, w_key, w_value, w_output):
    at = Lines()
    length, cols = tokens.shape
    width = w_query.shape[1]
    number = width // HD
    half = length // 2
    own = jnp.reshape(at.c, (1,)).astype(jnp.int32)

    token_a = gather_piece(at, tokens[:half], True)
    token_b = gather_piece(at, tokens[half:], True)
    last = [p for k, _, p in token_a if k == at.Z - 1][:1]
    cut = length * 5 // 8
    grad_a = gather_piece(at, out_grad[:cut], True, last)
    grad_b = gather_piece(at, out_grad[cut:], False, last)

    blank = jnp.zeros((length, cols * at.nh), BF16)
    whole_tokens = place(place(blank, token_a, 0, cols), token_b, half, cols)
    token_slices = slices_out(at, whole_tokens)
    query_lin = jnp.dot(whole_tokens, w_query, preferred_element_type=F32)
    key_lin = jnp.dot(whole_tokens, w_key, preferred_element_type=F32)
    value_lin = jnp.dot(whole_tokens, w_value, preferred_element_type=F32)

    columns = (length, width)
    square = (number * HD, HD)
    query_feat, key_feat, value_feat, scores, intra, local_kv = per_head(
        forward_kernel,
        number,
        [(query_lin, "c"), (key_lin, "c"), (value_lin, "c")],
        [(columns, BF16, "c")] * 3
        + [((number * length, length), BF16, "r"), (columns, F32, "c"), (square, BF16, "r")],
        flops=4 * length * length * width,
    )
    before = [at.across(local_kv, j) for j in range(1, at.nc)]
    normed, scale, attn_rows, prefix = per_head(
        functools.partial(norm_kernel, at.nc),
        number,
        [(intra, "c"), (query_feat, "c")] + [(b, "r") for b in before],
        [(columns, F32, "c"), (columns, F32, "c"), (columns, BF16, "c"), (square, BF16, "r")],
        (own,),
        flops=2 * length * HD * width,
    )
    rows_all = blocks_out(at, attn_rows)

    early = [[p for p in g if p[0] < at.Z - 1] for g in (grad_a, grad_b)]
    late = [[p for p in g if p[0] == at.Z - 1] for g in (grad_a, grad_b)]
    most_grads = place(place(blank, early[0], 0, cols), early[1], cut, cols)
    most_grads = tie(most_grads, attn_rows)
    grad_most = jnp.dot(most_grads, w_output, preferred_element_type=F32)
    whole_grads = place(place(most_grads, late[0], 0, cols), late[1], cut, cols)
    group = at.Y * cols
    start = ((at.z + 1) % at.Z) * group
    grad_last = jnp.dot(
        lax.dynamic_slice_in_dim(whole_grads, start, group, 1),
        lax.dynamic_slice_in_dim(w_output, start, group, 0),
        preferred_element_type=F32,
    )
    grad_slices = slices_out(at, whole_grads)
    out_delta, local_qg = per_head(
        delta_kernel,
        number,
        [(grad_most, "c"), (grad_last, "c"), (normed, "c"), (scale, "c"), (query_feat, "c")],
        [(columns, BF16, "c"), (square, BF16, "r")],
        flops=2 * length * HD * width,
    )
    after = [at.across(local_qg, j) for j in range(1, at.nc)]
    query_pre, inner_k, inner_v = per_head(
        inner_kernel,
        number,
        [(out_delta, "c"), (query_feat, "c"), (key_feat, "c"), (value_feat, "c")]
        + [(scores, "r"), (prefix, "r"), (query_lin, "c")],
        [(columns, BF16, "c"), (columns, F32, "c"), (columns, F32, "c")],
        flops=8 * length * length * width,
    )
    query_all = blocks_out(at, query_pre)
    (kv_pre,) = per_head(
        functools.partial(outer_kernel, at.nc),
        number,
        [(inner_k, "c"), (inner_v, "c"), (key_feat, "c"), (value_feat, "c"), (key_lin, "c")]
        + [(a, "r") for a in after],
        [((2, length, width), BF16, "h")],
        (own,),
        flops=4 * length * HD * width,
    )
    kv_pre, *token_slices = lax.optimization_barrier((kv_pre, *token_slices))
    kv_all = blocks_out(at, kv_pre)

    weights = (w_query, w_key, w_value)
    total = None
    for k in range(1, at.Z + 1):
        held = None
        for j in range(1, at.Y + 1):
            dtype = BF16 if j == 1 and j < at.Y else F32
            mine = part_of(at.shard(k, j), query_pre, kv_pre, weights, cols, dtype)
            if held is not None:
                mine = [m + h.astype(F32) for m, h in zip(mine, held)]
            held = mine
            if j < at.Y:
                held = [at.along_y(h.astype(BF16)) for h in held]
        if total is not None:
            held = [h + t.astype(F32) for h, t in zip(held, total)]
        total = [h.astype(BF16) for h in held]
        if k < at.Z:
            total = [at.along_z(t) for t in total]
    input_grad = jnp.concatenate(total, axis=0)

    def contract(left, right):
        return jnp.einsum("td,ti->di", left, right, preferred_element_type=F32).astype(BF16)

    tokens_cat = jnp.concatenate(token_slices, axis=0)
    grad_query = contract(tokens_cat, jnp.concatenate(query_all, axis=0))
    kv_cat = jnp.concatenate(kv_all, axis=1)
    grad_key = contract(tokens_cat, kv_cat[0])
    grad_value = contract(tokens_cat, kv_cat[1])
    grad_output = contract(
        jnp.concatenate(grad_slices, axis=0), jnp.concatenate(rows_all, axis=0)
    )
    return (input_grad, grad_query, grad_key, grad_value, grad_output)


def solution(mesh):
    return jax.shard_map(
        local,
        mesh=mesh,
        in_specs=(P("ctx", "head"),) * 2 + (P(None, "head"),) * 4,
        out_specs=(P("ctx", "head"),) * 5,
        check_vma=False,
    )
```

```python
import functools

import jax
import jax.numpy as jnp
from jax import lax
from jax.experimental import pallas as pl
from jax.experimental.pallas import tpu as pltpu
from jax.sharding import PartitionSpec as P

HD = 128
F32 = jnp.float32
BF16 = jnp.bfloat16


def tie(x, *others):
    return lax.optimization_barrier((x,) + others)[0]


class Lines:
    def __init__(self):
        self.nh = lax.axis_size("head")
        self.nc = lax.axis_size("ctx")
        self.Z = 4 if self.nh % 4 == 0 else 1
        self.Y = self.nh // self.Z
        here = lax.axis_index("head")
        self.c = lax.axis_index("ctx")
        self.z = here // self.Y
        self.y = here % self.Y

    def along_z(self, x):
        return lax.ppermute(x, "head", [(i, (i + self.Y) % self.nh) for i in range(self.nh)])

    def along_y(self, x):
        Y = self.Y
        return lax.ppermute(x, "head", [(i, i // Y * Y + (i + 1) % Y) for i in range(self.nh)])

    def swap_z(self, x):
        Y = self.Y
        return lax.ppermute(x, "head", [(i, (i // Y ^ 1) * Y + i % Y) for i in range(self.nh)])

    def across(self, x, j):
        return lax.ppermute(x, "ctx", [(i, i ^ j) for i in range(self.nc)])

    def shard(self, k, j):
        return ((self.z - k) % self.Z) * self.Y + (self.y - j) % self.Y


def gather_piece(at, x, z_first, after=()):
    parts = []
    if z_first:
        now = x
        for k in range(at.Z):
            if k:
                now = at.along_z(tie(now, *after) if after and k == 1 else now)
            side = now
            for j in range(at.Y):
                if j:
                    side = at.along_y(side)
                parts.append((k, at.shard(k, j), side))
        return parts
    sides = [x]
    for _ in range(at.Y - 1):
        sides.append(at.along_y(sides[-1]))
    now = jnp.concatenate(sides, axis=1)
    cols = x.shape[1]
    for k in range(at.Z):
        if k:
            now = at.along_z(tie(now, *after) if after and k == 1 else now)
        for j in range(at.Y):
            parts.append((k, at.shard(k, j), now[:, j * cols : (j + 1) * cols]))
    return parts


def place(whole, parts, row, cols):
    for _, where, part in parts:
        whole = lax.dynamic_update_slice(whole, part, (row, where * cols))
    return whole


def slices_out(at, whole, *after):
    width = whole.shape[1] // at.nc
    half = whole.shape[0] // 2
    out, far = [], []
    for j in range(at.nc):
        piece = lax.dynamic_slice_in_dim(whole, (at.c ^ j) * width, width, 1)
        if j < 2:
            out.append(at.across(tie(piece, *after), j) if j else piece)
            continue
        for part in (piece[:half], piece[half:]):
            far.append(at.across(tie(part, *after, *far[-1:]), j))
        out.extend(far[-2:])
    return out, far


def slices_shared(at, whole):
    width = whole.shape[1] // at.nc
    half = whole.shape[0] // 2
    mine = (at.z % 2) * half
    out, far = [], []
    for j in range(at.nc):
        start = (at.c ^ j) * width
        if j < 2 or at.Z % 2:
            piece = lax.dynamic_slice_in_dim(whole, start, width, 1)
            out.append(at.across(piece, j) if j else piece)
            continue
        piece = lax.dynamic_slice(whole, (mine, start), (half, width))
        piece = at.across(tie(piece, *far[-1:]) if far else piece, j)
        far.append(piece)
        other = at.swap_z(piece)
        both = jnp.zeros((2 * half, width), whole.dtype)
        both = lax.dynamic_update_slice(both, piece, (mine, 0))
        out.append(lax.dynamic_update_slice(both, other, (half - mine, 0)))
    return out, far


def blocks_out(at, x):
    have = {0: x}
    bit = at.nc // 2
    while bit:
        have.update({j | bit: at.across(v, bit) for j, v in list(have.items())})
        bit //= 2
    return [have[j] for j in range(at.nc)]


def mm(a, b, ca, cb):
    return lax.dot_general(a, b, (((ca,), (cb,)), ((), ())), preferred_element_type=F32)


def slope(values):
    return jnp.where(values > 0, 1.0, jnp.exp(jnp.minimum(values, 0.0)))


def feature(values):
    return jnp.where(values > 0, values + 1.0, jnp.exp(jnp.minimum(values, 0.0)))


def causal(values):
    rows = lax.broadcasted_iota(jnp.int32, values.shape, 0)
    cols = lax.broadcasted_iota(jnp.int32, values.shape, 1)
    return jnp.where(rows >= cols, values, 0.0)


def whole_call(kernel, ins, outs, scalars=()):
    vmem = pl.BlockSpec(memory_space=pltpu.VMEM)
    return pl.pallas_call(
        kernel,
        out_shape=[jax.ShapeDtypeStruct(s, d) for s, d in outs],
        in_specs=[pl.BlockSpec(memory_space=pltpu.SMEM)] * len(scalars) + [vmem] * len(ins),
        out_specs=[vmem] * len(outs),
        compiler_params=pltpu.CompilerParams(vmem_limit_bytes=32 * 1024 * 1024),
        cost_estimate=pl.CostEstimate(flops=1000, bytes_accessed=1000, transcendentals=0),
    )(*scalars, *ins)


def heads(array):
    return [slice(i * HD, (i + 1) * HD) for i in range(array.shape[1] // HD)]


def forward_kernel(*refs):
    qa_ref, ka_ref, va_ref, qb_ref, kb_ref, vb_ref, q_ref, k_ref = refs[:8]
    qf_ref, kf_ref, vf_ref, sc_ref, in_ref, kv_ref = refs[8:]
    for i, at in enumerate(heads(q_ref)):
        query_lin = qa_ref[:, at] + qb_ref[:, at]
        key_lin = ka_ref[:, at] + kb_ref[:, at]
        q_ref[:, at] = query_lin
        k_ref[:, at] = key_lin
        qf = feature(query_lin).astype(BF16)
        kf = feature(key_lin).astype(BF16)
        vf = (va_ref[:, at] + vb_ref[:, at]).astype(BF16)
        scores = causal(mm(qf, kf, 1, 1)).astype(BF16)
        qf_ref[:, at] = qf
        kf_ref[:, at] = kf
        vf_ref[:, at] = vf
        sc_ref[i] = scores
        in_ref[:, at] = mm(scores, vf, 1, 0)
        kv_ref[at, :] = mm(kf, vf, 0, 0).astype(BF16)


def state_sum(c, refs, at, later):
    total = jnp.zeros((HD, HD), F32)
    for j, ref in enumerate(refs):
        other = c ^ (j + 1)
        use = (other > c) if later else (other < c)
        total = total + jnp.where(use, ref[at, :].astype(F32), 0.0)
    return total.astype(BF16)


def norm_kernel(nc, c_ref, in_ref, qf_ref, *refs):
    kv, (no_ref, sl_ref, ar_ref, pf_ref) = refs[: nc - 1], refs[nc - 1 :]
    for at in heads(qf_ref):
        prefix = state_sum(c_ref[0], kv, at, False)
        attended = in_ref[:, at] + mm(qf_ref[:, at], prefix, 1, 0)
        scale = lax.rsqrt(jnp.mean(attended * attended, axis=1, keepdims=True) + 1e-06)
        normed = attended * scale
        no_ref[:, at] = normed
        sl_ref[:, at] = jnp.broadcast_to(scale, normed.shape)
        ar_ref[:, at] = normed.astype(BF16)
        pf_ref[at, :] = prefix


def delta_kernel(ga_ref, gb_ref, no_ref, sl_ref, qf_ref, od_ref, qg_ref):
    for at in heads(qf_ref):
        grad = ga_ref[:, at] + gb_ref[:, at]
        normed = no_ref[:, at]
        mean = jnp.mean(grad * normed, axis=1, keepdims=True)
        delta = (sl_ref[:, at] * (grad - normed * mean)).astype(BF16)
        od_ref[:, at] = delta
        qg_ref[at, :] = mm(qf_ref[:, at], delta, 0, 0).astype(BF16)


def inner_kernel(
    od_ref, qf_ref, kf_ref, vf_ref, sc_ref, pf_ref, q_ref, qp_ref, qt_ref, fk_ref, fv_ref
):
    for i, at in enumerate(heads(qf_ref)):
        delta = od_ref[:, at]
        score_grad = causal(mm(delta, vf_ref[:, at], 1, 1)).astype(BF16)
        feat_q = mm(score_grad, kf_ref[:, at], 1, 0) + mm(delta, pf_ref[at, :], 1, 1)
        pre = feat_q * slope(q_ref[:, at])
        qp_ref[:, at] = pre.astype(BF16)
        qt_ref[at, :] = pre.T.astype(BF16)
        fk_ref[:, at] = mm(score_grad, qf_ref[:, at], 0, 0)
        fv_ref[:, at] = mm(sc_ref[i], delta, 0, 0)


def outer_kernel(nc, c_ref, fk_ref, fv_ref, kf_ref, vf_ref, k_ref, *refs):
    qg, (kv_ref, kt_ref) = refs[: nc - 1], refs[nc - 1 :]
    for at in heads(kf_ref):
        suffix = state_sum(c_ref[0], qg, at, True)
        feat_k = fk_ref[:, at] + mm(vf_ref[:, at], suffix, 1, 1)
        feat_v = fv_ref[:, at] + mm(kf_ref[:, at], suffix, 1, 0)
        key_pre = feat_k * slope(k_ref[:, at])
        kv_ref[0, :, at] = key_pre.astype(BF16)
        kv_ref[1, :, at] = feat_v.astype(BF16)
        kt_ref[0, at, :] = key_pre.T.astype(BF16)
        kt_ref[1, at, :] = feat_v.T.astype(BF16)


def part_kernel(count, s_ref, q_ref, kv_ref, wq_ref, wk_ref, wv_ref, *out_refs):
    total = mm(wq_ref[...], q_ref[...], 1, 0)
    total = total + mm(wk_ref[...], kv_ref[0], 1, 0)
    total = total + mm(wv_ref[...], kv_ref[1], 1, 0)
    for n, out_ref in enumerate(out_refs):

        @pl.when(pl.program_id(0) // count == n)
        def _():
            out_ref[...] = total.astype(out_ref.dtype)


def parts_of(places, query_turned, kv_turned, weights, cols, dtype):
    width, rows = query_turned.shape
    tile = min(512, cols)
    count = cols // tile
    weight = pl.BlockSpec((tile, width), lambda i, s: (s[i // count] * count + i % count, 0))

    def out(n):
        return pl.BlockSpec((tile, rows), lambda i, s: (jnp.clip(i - n * count, 0, count - 1), 0))

    return pl.pallas_call(
        functools.partial(part_kernel, count),
        out_shape=[jax.ShapeDtypeStruct((cols, rows), dtype)] * len(places),
        grid_spec=pltpu.PrefetchScalarGridSpec(
            num_scalar_prefetch=1,
            grid=(len(places) * count,),
            in_specs=[
                pl.BlockSpec((width, rows), lambda i, s: (0, 0)),
                pl.BlockSpec((2, width, rows), lambda i, s: (0, 0, 0)),
                weight,
                weight,
                weight,
            ],
            out_specs=[out(n) for n in range(len(places))],
        ),
        compiler_params=pltpu.CompilerParams(vmem_limit_bytes=32 * 1024 * 1024),
        cost_estimate=pl.CostEstimate(flops=1000, bytes_accessed=1000, transcendentals=0),
    )(jnp.stack(places).astype(jnp.int32), query_turned, kv_turned, *weights)


def local(tokens, out_grad, w_query, w_key, w_value, w_output):
    at = Lines()
    length, cols = tokens.shape
    width = w_query.shape[1]
    number = width // HD
    half = length // 2
    own = jnp.reshape(at.c, (1,)).astype(jnp.int32)

    tokens_in = gather_piece(at, tokens, True)
    cut = length * 5 // 8
    grads_a = gather_piece(at, out_grad[:cut], True)
    grads_b = gather_piece(at, out_grad[cut:], False)

    def split(parts):
        return [p for p in parts if p[0] < at.Z - 1], [p for p in parts if p[0] == at.Z - 1]

    group = at.Y * cols
    start = ((at.z + 1) % at.Z) * group

    def last_dot(whole, w):
        return jnp.dot(
            lax.dynamic_slice_in_dim(whole, start, group, 1),
            lax.dynamic_slice_in_dim(w, start, group, 0),
            preferred_element_type=F32,
        )
    blank = jnp.zeros((length, cols * at.nh), BF16)
    early, late = split(tokens_in)
    most_tokens = place(blank, early, 0, cols)
    ready_tokens = tie(most_tokens, split(grads_a)[1][0][2], split(grads_b)[1][0][2])
    most_lin = [
        jnp.dot(ready_tokens, w, preferred_element_type=F32) for w in (w_query, w_key, w_value)
    ]
    whole_tokens = place(tie(ready_tokens, *most_lin), late, 0, cols)
    last_lin = [last_dot(whole_tokens, w) for w in (w_query, w_key, w_value)]
    token_slices, far = slices_shared(at, whole_tokens)

    columns = (length, width)
    square = (number * HD, HD)
    query_lin, key_lin, query_feat, key_feat, value_feat, scores, intra, local_kv = whole_call(
        forward_kernel,
        [*most_lin, tie(last_lin[0], *far[:1]), *last_lin[1:]],
        [(columns, F32)] * 2
        + [(columns, BF16)] * 3
        + [((number, length, length), BF16), (columns, F32), (square, BF16)],
    )
    before = [at.across(local_kv, j) for j in range(1, at.nc)]
    (early_a, late_a), (early_b, late_b) = split(grads_a), split(grads_b)
    most_grads = place(place(blank, early_a, 0, cols), early_b, cut, cols)
    grad_most = jnp.dot(most_grads, w_output, preferred_element_type=F32)
    normed, scale, attn_rows, prefix = whole_call(
        functools.partial(norm_kernel, at.nc),
        [tie(intra, *far[1:]), query_feat, *before],
        [(columns, F32), (columns, F32), (columns, BF16), (square, BF16)],
        (own,),
    )
    rows_all = blocks_out(at, attn_rows)

    whole_grads = place(tie(most_grads, grad_most), late_a, 0, cols)
    whole_grads = place(whole_grads, late_b, cut, cols)
    grad_last = last_dot(whole_grads, w_output)
    out_delta, local_qg = whole_call(
        delta_kernel,
        [grad_most, grad_last, normed, scale, query_feat],
        [(columns, BF16), (square, BF16)],
    )
    after = [at.across(local_qg, j) for j in range(1, at.nc)]
    query_pre, query_turned, inner_k, inner_v = whole_call(
        inner_kernel,
        [out_delta, query_feat, key_feat, value_feat, scores, prefix, query_lin],
        [(columns, BF16), ((width, length), BF16), (columns, F32), (columns, F32)],
    )
    query_all = blocks_out(at, query_pre)
    kv_pre, kv_turned = whole_call(
        functools.partial(outer_kernel, at.nc),
        [inner_k, inner_v, key_feat, value_feat, key_lin, *after],
        [((2, length, width), BF16), ((2, width, length), BF16)],
        (own,),
    )
    kv_all = blocks_out(at, kv_pre)
    far_pre = query_all[2:3] + kv_all[2:3]
    grad_slices, far = slices_out(at, whole_grads, kv_pre, *far_pre)

    weights = (w_query, w_key, w_value)

    def parts(j, dtype):
        places = [at.shard(k, j) for k in range(1, at.Z + 1)]
        return parts_of(places, query_turned, kv_turned, weights, cols, dtype)

    def halves(x):
        return [x[: cols // 2].astype(F32), x[cols // 2 :].astype(F32)]

    sides = None
    for j in range(1, at.Y):
        mine = parts(j, BF16 if j == 1 else F32)
        if sides is not None:
            mine = [(m + s.astype(F32)).astype(BF16) for m, s in zip(mine, sides)]
        sides = [at.along_y(m) for m in mine]
    mine = parts(at.Y, F32)
    total = None
    for k in range(1, at.Z + 1):
        held = halves(mine[k - 1])
        due = [f for i, f in enumerate(far) if i * at.Z // len(far) + 2 == k]
        due = due + far_pre if k == 1 else due
        if due:
            held = lax.optimization_barrier((*held, *due))[:2]
        if sides is not None:
            held = [h + s for h, s in zip(held, halves(sides[k - 1]))]
        if total is not None:
            held = [h + t.astype(F32) for h, t in zip(held, total)]
        total = [h.astype(BF16) for h in held]
        if k < at.Z:
            total = [at.along_z(t) for t in total]
        if k == max(at.Z - 2, 1):
            free = total
    total = lax.optimization_barrier((*total, *far))[:2]
    input_grad = jnp.concatenate(total, axis=0).T

    def contract(left, right):
        return jnp.einsum("td,ti->di", left, right, preferred_element_type=F32).astype(BF16)

    tokens_cat = tie(jnp.concatenate(token_slices, axis=0), *free)
    grad_query = contract(tokens_cat, jnp.concatenate(query_all, axis=0))
    kv_cat = jnp.concatenate(kv_all, axis=1)
    grad_key = contract(tokens_cat, kv_cat[0])
    grad_value = contract(tokens_cat, kv_cat[1])
    grad_output = contract(
        jnp.concatenate(grad_slices, axis=0), jnp.concatenate(rows_all, axis=0)
    )
    return (input_grad, grad_query, grad_key, grad_value, grad_output)


def solution(mesh):
    return jax.shard_map(
        local,
        mesh=mesh,
        in_specs=(P("ctx", "head"),) * 2 + (P(None, "head"),) * 4,
        out_specs=(P("ctx", "head"),) * 5,
        check_vma=False,
    )
```

```python
import functools

import jax
import jax.numpy as jnp
from jax import lax
from jax.experimental import pallas as pl
from jax.experimental.pallas import tpu as pltpu
from jax.sharding import PartitionSpec as P

HD = 128
F32 = jnp.float32
BF16 = jnp.bfloat16


def tie(x, *others):
    return lax.optimization_barrier((x,) + others)[0]


class Lines:
    def __init__(self):
        self.nh = lax.axis_size("head")
        self.nc = lax.axis_size("ctx")
        self.Z = 4 if self.nh % 4 == 0 else 1
        self.Y = self.nh // self.Z
        here = lax.axis_index("head")
        self.c = lax.axis_index("ctx")
        self.z = here // self.Y
        self.y = here % self.Y

    def along_z(self, x):
        return lax.ppermute(x, "head", [(i, (i + self.Y) % self.nh) for i in range(self.nh)])

    def along_y(self, x):
        Y = self.Y
        return lax.ppermute(x, "head", [(i, i // Y * Y + (i + 1) % Y) for i in range(self.nh)])

    def swap_z(self, x):
        Y = self.Y
        return lax.ppermute(x, "head", [(i, (i // Y ^ 1) * Y + i % Y) for i in range(self.nh)])

    def across(self, x, j):
        return lax.ppermute(x, "ctx", [(i, i ^ j) for i in range(self.nc)])

    def shard(self, k, j):
        return ((self.z - k) % self.Z) * self.Y + (self.y - j) % self.Y


def gather_piece(at, x, z_first, after=()):
    parts = []
    if z_first:
        now = x
        for k in range(at.Z):
            if k:
                now = at.along_z(now)
            side = tie(now, *after) if k == at.Z - 1 else now
            for j in range(at.Y):
                if j:
                    side = at.along_y(side)
                parts.append((k, at.shard(k, j), side))
        return parts
    sides = [x]
    for _ in range(at.Y - 1):
        sides.append(at.along_y(sides[-1]))
    now = jnp.concatenate(sides, axis=1)
    cols = x.shape[1]
    for k in range(at.Z):
        if k:
            now = at.along_z(tie(now, *after) if k == at.Z - 1 else now)
        for j in range(at.Y):
            parts.append((k, at.shard(k, j), now[:, j * cols : (j + 1) * cols]))
    return parts


def place(whole, parts, row, cols):
    for _, where, part in parts:
        whole = lax.dynamic_update_slice(whole, part, (row, where * cols))
    return whole


def slices_of(at, whole, shared, *after):
    rows = whole.shape[0]
    width = whole.shape[1] // at.nc
    shared = shared and at.Z % 2 == 0
    half = rows // 2 if shared else rows
    mine = (at.z % 2) * half if shared else 0

    def piece(j, start, count):
        return lax.dynamic_slice(whole, (start, (at.c ^ j) * width), (count, width))

    out = [piece(0, 0, rows), at.across(tie(piece(1, 0, rows), *after), 1)]
    far = []
    for j in range(2, at.nc, 2):
        both = jnp.stack([piece(j, mine, half), piece(j + 1, mine, half)])
        both = at.across(tie(both, *after, *far[-1:]), j)
        far.append(both)
        if shared:
            full = jnp.zeros((2, rows, width), whole.dtype)
            full = lax.dynamic_update_slice(full, both, (0, mine, 0))
            both = lax.dynamic_update_slice(full, at.swap_z(both), (0, half - mine, 0))
        out += [both[0], at.across(both[1], 1)]
    return out, far


def blocks_out(at, x):
    have = {0: x}
    bit = at.nc // 2
    while bit:
        have.update({j | bit: at.across(v, bit) for j, v in list(have.items())})
        bit //= 2
    return [have[j] for j in range(at.nc)]


def mm(a, b, ca, cb):
    return lax.dot_general(a, b, (((ca,), (cb,)), ((), ())), preferred_element_type=F32)


def slope(values):
    return jnp.where(values > 0, 1.0, jnp.exp(jnp.minimum(values, 0.0)))


def feature(values):
    return jnp.where(values > 0, values + 1.0, jnp.exp(jnp.minimum(values, 0.0)))


def causal(values):
    rows = lax.broadcasted_iota(jnp.int32, values.shape, 0)
    cols = lax.broadcasted_iota(jnp.int32, values.shape, 1)
    return jnp.where(rows >= cols, values, 0.0)


def whole_call(kernel, ins, outs, scalars=()):
    vmem = pl.BlockSpec(memory_space=pltpu.VMEM)
    return pl.pallas_call(
        kernel,
        out_shape=[jax.ShapeDtypeStruct(s, d) for s, d in outs],
        in_specs=[pl.BlockSpec(memory_space=pltpu.SMEM)] * len(scalars) + [vmem] * len(ins),
        out_specs=[vmem] * len(outs),
        compiler_params=pltpu.CompilerParams(vmem_limit_bytes=32 * 1024 * 1024),
        cost_estimate=pl.CostEstimate(flops=1000, bytes_accessed=1000, transcendentals=0),
    )(*scalars, *ins)


def heads(array):
    return [slice(i * HD, (i + 1) * HD) for i in range(array.shape[1] // HD)]


def forward_kernel(*refs):
    qa_ref, ka_ref, va_ref, qb_ref, kb_ref, vb_ref, q_ref, k_ref = refs[:8]
    qf_ref, kf_ref, vf_ref, sc_ref, in_ref, kv_ref = refs[8:]
    for i, at in enumerate(heads(q_ref)):
        query_lin = qa_ref[:, at] + qb_ref[:, at]
        key_lin = ka_ref[:, at] + kb_ref[:, at]
        q_ref[:, at] = query_lin
        k_ref[:, at] = key_lin
        qf = feature(query_lin).astype(BF16)
        kf = feature(key_lin).astype(BF16)
        vf = (va_ref[:, at] + vb_ref[:, at]).astype(BF16)
        scores = causal(mm(qf, kf, 1, 1)).astype(BF16)
        qf_ref[:, at] = qf
        kf_ref[:, at] = kf
        vf_ref[:, at] = vf
        sc_ref[i] = scores
        in_ref[:, at] = mm(scores, vf, 1, 0)
        kv_ref[at, :] = mm(kf, vf, 0, 0).astype(BF16)


def state_sum(c, refs, at, later):
    total = jnp.zeros((HD, HD), F32)
    for j, ref in enumerate(refs):
        other = c ^ (j + 1)
        use = (other > c) if later else (other < c)
        total = total + jnp.where(use, ref[at, :].astype(F32), 0.0)
    return total.astype(BF16)


def norm_kernel(nc, c_ref, in_ref, qf_ref, *refs):
    kv, (no_ref, sl_ref, ar_ref, pf_ref) = refs[: nc - 1], refs[nc - 1 :]
    for at in heads(qf_ref):
        prefix = state_sum(c_ref[0], kv, at, False)
        attended = in_ref[:, at] + mm(qf_ref[:, at], prefix, 1, 0)
        scale = lax.rsqrt(jnp.mean(attended * attended, axis=1, keepdims=True) + 1e-06)
        normed = attended * scale
        no_ref[:, at] = normed
        sl_ref[:, at] = jnp.broadcast_to(scale, normed.shape)
        ar_ref[:, at] = normed.astype(BF16)
        pf_ref[at, :] = prefix


def delta_kernel(ga_ref, gb_ref, no_ref, sl_ref, qf_ref, od_ref, qg_ref):
    for at in heads(qf_ref):
        grad = ga_ref[:, at] + gb_ref[:, at]
        normed = no_ref[:, at]
        mean = jnp.mean(grad * normed, axis=1, keepdims=True)
        delta = (sl_ref[:, at] * (grad - normed * mean)).astype(BF16)
        od_ref[:, at] = delta
        qg_ref[at, :] = mm(qf_ref[:, at], delta, 0, 0).astype(BF16)


def inner_kernel(
    od_ref, qf_ref, kf_ref, vf_ref, sc_ref, pf_ref, q_ref, qp_ref, qt_ref, fk_ref, fv_ref
):
    for i, at in enumerate(heads(qf_ref)):
        delta = od_ref[:, at]
        score_grad = causal(mm(delta, vf_ref[:, at], 1, 1)).astype(BF16)
        feat_q = mm(score_grad, kf_ref[:, at], 1, 0) + mm(delta, pf_ref[at, :], 1, 1)
        pre = feat_q * slope(q_ref[:, at])
        qp_ref[:, at] = pre.astype(BF16)
        qt_ref[at, :] = pre.T.astype(BF16)
        fk_ref[:, at] = mm(score_grad, qf_ref[:, at], 0, 0)
        fv_ref[:, at] = mm(sc_ref[i], delta, 0, 0)


def outer_kernel(nc, c_ref, fk_ref, fv_ref, kf_ref, vf_ref, k_ref, *refs):
    qg, (kv_ref, kt_ref) = refs[: nc - 1], refs[nc - 1 :]
    for at in heads(kf_ref):
        suffix = state_sum(c_ref[0], qg, at, True)
        feat_k = fk_ref[:, at] + mm(vf_ref[:, at], suffix, 1, 1)
        feat_v = fv_ref[:, at] + mm(kf_ref[:, at], suffix, 1, 0)
        key_pre = feat_k * slope(k_ref[:, at])
        kv_ref[0, :, at] = key_pre.astype(BF16)
        kv_ref[1, :, at] = feat_v.astype(BF16)
        kt_ref[0, at, :] = key_pre.T.astype(BF16)
        kt_ref[1, at, :] = feat_v.T.astype(BF16)


def part_kernel(count, s_ref, q_ref, kv_ref, wq_ref, wk_ref, wv_ref, *out_refs):
    total = mm(wq_ref[...], q_ref[...], 1, 0)
    total = total + mm(wk_ref[...], kv_ref[0], 1, 0)
    total = total + mm(wv_ref[...], kv_ref[1], 1, 0)
    for n, out_ref in enumerate(out_refs):

        @pl.when(pl.program_id(0) // count == n)
        def _():
            out_ref[...] = total.astype(out_ref.dtype)


def parts_of(places, query_turned, kv_turned, weights, cols, dtype):
    width, rows = query_turned.shape
    tile = min(512, cols)
    count = cols // tile
    weight = pl.BlockSpec((tile, width), lambda i, s: (s[i // count] * count + i % count, 0))

    def out(n):
        return pl.BlockSpec((tile, rows), lambda i, s: (jnp.clip(i - n * count, 0, count - 1), 0))

    return pl.pallas_call(
        functools.partial(part_kernel, count),
        out_shape=[jax.ShapeDtypeStruct((cols, rows), dtype)] * len(places),
        grid_spec=pltpu.PrefetchScalarGridSpec(
            num_scalar_prefetch=1,
            grid=(len(places) * count,),
            in_specs=[
                pl.BlockSpec((width, rows), lambda i, s: (0, 0)),
                pl.BlockSpec((2, width, rows), lambda i, s: (0, 0, 0)),
                weight,
                weight,
                weight,
            ],
            out_specs=[out(n) for n in range(len(places))],
        ),
        compiler_params=pltpu.CompilerParams(vmem_limit_bytes=32 * 1024 * 1024),
        cost_estimate=pl.CostEstimate(flops=1000, bytes_accessed=1000, transcendentals=0),
    )(jnp.stack(places).astype(jnp.int32), query_turned, kv_turned, *weights)


def local(tokens, out_grad, w_query, w_key, w_value, w_output):
    at = Lines()
    length, cols = tokens.shape
    width = w_query.shape[1]
    number = width // HD
    half = length // 2
    own = jnp.reshape(at.c, (1,)).astype(jnp.int32)

    tokens_in = gather_piece(at, tokens, True)
    def split(parts):
        return [p for p in parts if p[0] < at.Z - 1], [p for p in parts if p[0] == at.Z - 1]

    group = at.Y * cols
    start = ((at.z + 1) % at.Z) * group

    def last_dot(whole, w):
        return jnp.dot(
            lax.dynamic_slice_in_dim(whole, start, group, 1),
            lax.dynamic_slice_in_dim(w, start, group, 0),
            preferred_element_type=F32,
        )
    blank = jnp.zeros((length, cols * at.nh), BF16)
    early, late = split(tokens_in)
    most_tokens = place(blank, early, 0, cols)
    most_lin = [
        jnp.dot(most_tokens, w, preferred_element_type=F32) for w in (w_query, w_key, w_value)
    ]
    cut = length * 5 // 8
    grads_a = gather_piece(at, out_grad[:cut], True, most_lin)
    grads_b = gather_piece(at, out_grad[cut:], False, most_lin)
    whole_tokens = place(tie(most_tokens, *most_lin), late, 0, cols)
    last_lin = [last_dot(whole_tokens, w) for w in (w_query, w_key, w_value)]
    token_slices, far = slices_of(at, whole_tokens, True)

    columns = (length, width)
    square = (number * HD, HD)
    query_lin, key_lin, query_feat, key_feat, value_feat, scores, intra, local_kv = whole_call(
        forward_kernel,
        [*most_lin, *last_lin],
        [(columns, F32)] * 2
        + [(columns, BF16)] * 3
        + [((number, length, length), BF16), (columns, F32), (square, BF16)],
    )
    before = [at.across(local_kv, j) for j in range(1, at.nc)]
    (early_a, late_a), (early_b, late_b) = split(grads_a), split(grads_b)
    most_grads = place(place(blank, early_a, 0, cols), early_b, cut, cols)
    most_grads = tie(most_grads, local_kv)
    grad_most = jnp.dot(most_grads, w_output, preferred_element_type=F32)
    normed, scale, attn_rows, prefix = whole_call(
        functools.partial(norm_kernel, at.nc),
        [intra, query_feat, *before],
        [(columns, F32), (columns, F32), (columns, BF16), (square, BF16)],
        (own,),
    )
    rows_all = blocks_out(at, attn_rows)

    whole_grads = place(tie(most_grads, grad_most), late_a, 0, cols)
    whole_grads = place(whole_grads, late_b, cut, cols)
    grad_last = last_dot(whole_grads, w_output)
    out_delta, local_qg = whole_call(
        delta_kernel,
        [tie(grad_most, *far), grad_last, normed, scale, query_feat],
        [(columns, BF16), (square, BF16)],
    )
    after = [at.across(local_qg, j) for j in range(1, at.nc)]
    query_pre, query_turned, inner_k, inner_v = whole_call(
        inner_kernel,
        [out_delta, query_feat, key_feat, value_feat, scores, prefix, query_lin],
        [(columns, BF16), ((width, length), BF16), (columns, F32), (columns, F32)],
    )
    query_all = blocks_out(at, query_pre)
    kv_pre, kv_turned = whole_call(
        functools.partial(outer_kernel, at.nc),
        [inner_k, inner_v, key_feat, value_feat, key_lin, *after],
        [((2, length, width), BF16), ((2, width, length), BF16)],
        (own,),
    )
    kv_all = blocks_out(at, kv_pre)
    far_pre = query_all[2:3] + kv_all[2:3]
    grad_slices, far = slices_of(at, tie(whole_grads, local_qg), False, kv_pre, *far_pre)

    weights = (w_query, w_key, w_value)

    def parts(j, dtype):
        places = [at.shard(k, j) for k in range(1, at.Z + 1)]
        return parts_of(places, query_turned, kv_turned, weights, cols, dtype)

    def halves(x):
        return [x[: cols // 2].astype(F32), x[cols // 2 :].astype(F32)]

    sides = None
    for j in range(1, at.Y):
        mine = parts(j, BF16 if j == 1 else F32)
        if sides is not None:
            mine = [(m + s.astype(F32)).astype(BF16) for m, s in zip(mine, sides)]
        sides = [at.along_y(m) for m in mine]
    mine = parts(at.Y, F32)
    total = None
    for k in range(1, at.Z + 1):
        held = halves(mine[k - 1])
        if k == min(2, at.Z):
            held = lax.optimization_barrier((*held, *far_pre))[:2]
        if sides is not None:
            held = [h + s for h, s in zip(held, halves(sides[k - 1]))]
        if total is not None:
            held = [h + t.astype(F32) for h, t in zip(held, total)]
        total = [h.astype(BF16) for h in held]
        if k < at.Z:
            total = [at.along_z(t) for t in total]
        if k == max(at.Z - 2, 1):
            free = total
    total = lax.optimization_barrier((*total, *far))[:2]
    input_grad = jnp.concatenate(total, axis=0).T

    def contract(left, right):
        return jnp.einsum("td,ti->di", left, right, preferred_element_type=F32).astype(BF16)

    tokens_cat = tie(jnp.concatenate(token_slices, axis=0), *free)
    grad_query = contract(tokens_cat, jnp.concatenate(query_all, axis=0))
    kv_cat = jnp.concatenate(kv_all, axis=1)
    grad_key = contract(tokens_cat, kv_cat[0])
    grad_value = contract(tokens_cat, kv_cat[1])
    grad_output = contract(
        jnp.concatenate(grad_slices, axis=0), jnp.concatenate(rows_all, axis=0)
    )
    return (input_grad, grad_query, grad_key, grad_value, grad_output)


def solution(mesh):
    return jax.shard_map(
        local,
        mesh=mesh,
        in_specs=(P("ctx", "head"),) * 2 + (P(None, "head"),) * 4,
        out_specs=(P("ctx", "head"),) * 5,
        check_vma=False,
    )
```
